256 devices in a mesh: dir: 2 (over y_lo), loop: 32 (over x, z), pb: 4 (over y_hi, core).
Axes of the slice: x: 4, y: 4 (y_hi: 2, y_lo: 2; y = y_hi * 2 + y_lo), z: 8, core: 2. Of those that a mesh axis runs over, the one named last changes fastest.
Arguments:
- embeddings: bfloat16 [2, 49152, 1024], P('dir', ('loop', 'pb')), may hold values from -24 to 24
- block_mask: int32 [32, 32], replicated, may hold values from 0 to 1, as said below
Outputs:
- soft_neighbour: bfloat16 [2, 49152, 1024], P('dir', ('loop', 'pb'))
- margin: float32 [2, 49152], P('dir', ('loop', 'pb'))
The draws below stay inside these ranges and needn't reach their ends.
Inputs may be any that keep to these rules, and one draw needn't show every extreme that they name: block_mask[i, i] is 1; block_mask[i, j] is 0 where the cyclic distance between i and j, min((i - j) mod 32, (j - i) mod 32), exceeds 2; the number of scored blocks differs from row to row, and some row scores all 5 blocks of its band.
All inputs are finite; a program needn't handle non-finite values.
Results may differ from the reference program's by a relative error of at most 0.0045.
Values may be sent and summed in bfloat16 or wider, within the bound.
No kernel may reach another device: no remote copies, remote signals or barrier semaphores. Data moves between devices by JAX's collectives and lax.ppermute only.
A program may use at most 128 MiB of HBM per device.

```python
import math
import jax
import jax.numpy as jnp
from jax import lax

D = 1024
ROWS_DEV = 384
BAND = 2
NROWS = 49152
N_LOOP = 32
N_PB = 4


def draw_embeddings(key, part):
    key = jax.random.fold_in(key, 11)
    subkeys = jax.random.split(key, 1)
    all_rows = jax.random.normal(subkeys[0], (2, NROWS, D), jnp.float32)
    return jnp.clip(all_rows, -24.0, 24.0).astype(jnp.bfloat16)


def draw_block_mask(key, part):
    key = jax.random.fold_in(key, 23)
    subkeys = jax.random.split(key, 2)
    block_index = jnp.arange(N_LOOP, dtype=jnp.int32)
    forward_gap = (block_index[None, :] - block_index[:, None]) % N_LOOP
    distance = jnp.minimum(forward_gap, N_LOOP - forward_gap)
    fill_level = jax.random.randint(subkeys[0], (N_LOOP, 1), 1, 4, dtype=jnp.int32)
    fill_level = jnp.where(block_index[:, None] == 0, 4, fill_level)
    draw_value = jax.random.randint(subkeys[1], (N_LOOP, N_LOOP), 0, 4, dtype=jnp.int32)
    scored = (distance == 0) | (distance <= BAND) & (draw_value < fill_level)
    return scored.astype(jnp.int32)


def setup_inputs(seed: int = 0) -> dict:
    key_of = jax.random.split(jax.random.key(seed), 3)
    return {
        "embeddings": draw_embeddings(jax.random.fold_in(key_of[2], 71), 0),
        "block_mask": draw_block_mask(jax.random.fold_in(key_of[2], 71), 0),
    }


sharpness = 3.0

def one_side(queries, key_rows, mask_rows):
    block_rows = ROWS_DEV * N_PB
    block_count = N_LOOP
    reach_blocks = BAND
    feature_count = queries.shape[1]
    score_scale = sharpness / math.sqrt(feature_count)
    extended = jnp.concatenate([key_rows[(block_count - reach_blocks) * block_rows:], key_rows, key_rows[:reach_blocks * block_rows]], axis=0)
    band_length = (2 * reach_blocks + 1) * block_rows

    def per_block(block_index):
        first_row = block_index * block_rows
        query_block = lax.dynamic_slice_in_dim(queries, first_row, block_rows, 0)
        key_band = lax.dynamic_slice_in_dim(extended, first_row, band_length, 0)
        targets = (block_index + jnp.arange(-reach_blocks, reach_blocks + 1, dtype=jnp.int32)) % block_count
        mask_line = lax.dynamic_index_in_dim(mask_rows, block_index, 0, False)
        tile_flags = mask_line[targets]
        scored = jnp.repeat(tile_flags, block_rows, total_repeat_length=band_length) > 0
        scores = jnp.einsum('qd,kd->qk', query_block, key_band, preferred_element_type=jnp.float32) * score_scale
        row_max = lax.optimization_barrier(jnp.max(jnp.where(scored[None, :], scores, -jnp.inf), axis=1))
        weights = jnp.exp(jnp.where(scored[None, :], scores - row_max[:, None], -jnp.inf))
        totals = lax.optimization_barrier(jnp.sum(weights, axis=1))
        blended = jnp.dot(weights.astype(jnp.bfloat16), key_band, preferred_element_type=jnp.float32) / totals[:, None]
        return (blended.astype(jnp.bfloat16), row_max + jnp.log(totals))
    blended, log_totals = lax.map(per_block, jnp.arange(block_count, dtype=jnp.int32))
    return (blended.reshape(-1, feature_count), log_totals.reshape(-1))

def reference(embeddings, block_mask):
    forward, forward_lse = one_side(embeddings[0], embeddings[1], block_mask)
    backward, backward_lse = one_side(embeddings[1], embeddings[0], block_mask.T)
    score_scale = sharpness / math.sqrt(embeddings.shape[2])
    pair_score = lax.optimization_barrier(jnp.sum(embeddings[0].astype(jnp.float32) * embeddings[1].astype(jnp.float32), axis=1)) * score_scale
    margin = pair_score - 0.5 * (forward_lse + backward_lse)
    return (jnp.stack([forward, backward]), jnp.stack([margin, margin]))
```

```python
import functools
import math

import jax
import jax.numpy as jnp
from jax import lax
from jax.experimental import pallas as pl
from jax.experimental.pallas import tpu as pltpu
from jax.sharding import PartitionSpec as P

sharpness = 3.0
AXES = ("dir", "loop", "pb")


def moved(value, route):
    sides, blocks, slabs = (lax.axis_size(axis) for axis in AXES)
    pairs = []
    for side in range(sides):
        for block in range(blocks):
            for slab in range(slabs):
                half, core = divmod(slab, 2)
                side_to, block_to, half_to, core_to = route(side, block, half, core)
                target = (side_to * blocks + block_to % blocks) * slabs + half_to * 2 + core_to
                pairs.append(((side * blocks + block) * slabs + slab, target))
    return lax.ppermute(value, AXES, pairs)


def across_near(side, block, half, core):
    return 1 - side, block, half, core


def across_far(side, block, half, core):
    return 1 - side, block, 1 - half, core


def sibling(side, block, half, core):
    return side, block, half, 1 - core


def ahead(side, block, half, core):
    return side, block + (1 if core == 0 else -1), half, core


def behind(side, block, half, core):
    return side, block - (1 if core == 0 else -1), half, core


def attend_kernel(slab_count, first, last, score_scale, *refs):
    refs = list(refs)
    flag_ref = None if first else refs.pop(0)
    query_ref = refs.pop(0)
    slab_refs = [refs.pop(0) for _ in range(slab_count)]
    if not first:
        max_in, total_in, sum_in = (refs.pop(0) for _ in range(3))
    if first:
        max_ref, total_ref, sum_ref, pair_ref = (refs.pop(0) for _ in range(4))
    elif last:
        blended_ref, log_ref = (refs.pop(0) for _ in range(2))
        max_ref, total_ref, sum_ref = (refs.pop(0) for _ in range(3))
    else:
        max_ref, total_ref, sum_ref = (refs.pop(0) for _ in range(3))
    key_ref, copy_sems = refs
    rows = query_ref.shape[0]
    copies = []
    for index, slab_ref in enumerate(slab_refs):
        copy = pltpu.make_async_copy(
            slab_ref, key_ref.at[pl.ds(index * rows, rows)], copy_sems.at[index]
        )
        copy.start()
        copies.append(copy)
    if first:
        max_ref[...] = jnp.full(max_ref.shape, -1e30, jnp.float32)
        total_ref[...] = jnp.zeros(total_ref.shape, jnp.float32)
        sum_ref[...] = jnp.zeros(sum_ref.shape, jnp.float32)
    else:
        max_ref[...] = max_in[...]
        total_ref[...] = total_in[...]
        sum_ref[...] = sum_in[...]

    def absorb(group):
        keys = key_ref[pl.ds(group * 2 * rows, 2 * rows), :]
        scores = (
            lax.dot_general(
                query_ref[...], keys, (((1,), (1,)), ((), ())), preferred_element_type=jnp.float32
            )
            * score_scale
        )
        old_max = max_ref[...]
        new_max = jnp.maximum(old_max, jnp.max(scores, axis=1, keepdims=True))
        weights = jnp.exp(scores - new_max)
        correction = jnp.exp(old_max - new_max)
        max_ref[...] = new_max
        total_ref[...] = total_ref[...] * correction + jnp.sum(weights, axis=1, keepdims=True)
        sum_ref[...] = sum_ref[...] * correction + jnp.dot(
            weights.astype(jnp.bfloat16), keys, preferred_element_type=jnp.float32
        )

    for group in range(slab_count // 2):
        copies[2 * group].wait()
        copies[2 * group + 1].wait()
        if first:
            absorb(group)
        else:
            pl.when(flag_ref[group] > 0)(functools.partial(absorb, group))
    if first:
        pair_ref[...] = (
            jnp.sum(
                query_ref[...].astype(jnp.float32) * key_ref[:rows, :].astype(jnp.float32),
                axis=1,
                keepdims=True,
            )
            * score_scale
        ).T
    if last:
        total = total_ref[...]
        blended_ref[...] = (sum_ref[...] / total).astype(jnp.bfloat16)
        log_ref[...] = (max_ref[...] + jnp.log(total)).T


def attend(query, slabs, score_scale, flags=None, state=None, last=False):
    rows, width = query.shape
    first = state is None
    count = len(slabs)
    vmem = pl.BlockSpec(memory_space=pltpu.VMEM)
    held = [
        jax.ShapeDtypeStruct((rows, 1), jnp.float32),
        jax.ShapeDtypeStruct((rows, 1), jnp.float32),
        jax.ShapeDtypeStruct((rows, width), jnp.float32),
    ]
    line = jax.ShapeDtypeStruct((1, rows), jnp.float32)
    scratch = [
        pltpu.VMEM((count * rows, width), jnp.bfloat16),
        pltpu.SemaphoreType.DMA((count,)),
    ]
    if first:
        out = held + [line]
    elif last:
        out = [jax.ShapeDtypeStruct((rows, width), jnp.bfloat16), line]
        scratch = [pltpu.VMEM(a.shape, a.dtype) for a in held] + scratch
    else:
        out = held
    in_specs = ([] if first else [pl.BlockSpec(memory_space=pltpu.SMEM)]) + [vmem]
    in_specs += [pl.BlockSpec(memory_space=pl.ANY)] * count
    in_specs += [] if first else [vmem] * 3
    operands = ([] if first else [flags]) + [query] + list(slabs) + ([] if first else list(state))
    return pl.pallas_call(
        functools.partial(attend_kernel, count, first, last, score_scale),
        out_shape=out,
        in_specs=in_specs,
        out_specs=[vmem] * len(out),
        scratch_shapes=scratch,
        compiler_params=pltpu.CompilerParams(vmem_limit_bytes=28 * 2**20),
        cost_estimate=pl.CostEstimate(
            flops=4 * count * rows * rows * width,
            bytes_accessed=2 * (count + 1) * rows * width + 8 * rows * width,
            transcendentals=count * rows * rows,
        ),
    )(*operands)


def shards(embeddings, block_mask):
    own = embeddings[0]
    score_scale = sharpness / math.sqrt(own.shape[1])
    side = lax.axis_index("dir")
    block = lax.axis_index("loop")
    core = lax.axis_index("pb") % 2
    count = lax.axis_size("loop")
    lines = jnp.where(side == 0, block_mask, block_mask.T)
    line = lax.dynamic_index_in_dim(lines, block, 0, False)
    step = jnp.where(core == 0, 1, -1)

    def flag(offset):
        return line[(block + offset * step) % count]

    near = moved(own, across_near)
    far = moved(own, across_far)
    ahead_1 = moved(own, ahead)
    near_sib = moved(near, sibling)
    far_sib = moved(far, sibling)
    ahead_2 = moved(ahead_1, ahead)

    behind_1 = [moved(near, behind), moved(far, behind)]
    cross_1 = [moved(ahead_1, across_near), moved(ahead_1, across_far)]
    max_0, total_0, sum_0, pair_score = attend(own, [near, far, near_sib, far_sib], score_scale)

    behind_2 = [moved(slab, behind) for slab in behind_1]
    cross_2 = [moved(ahead_2, across_near), moved(ahead_2, across_far)]
    behind_1_sib = [moved(slab, sibling) for slab in behind_1]
    cross_1_sib = [moved(slab, sibling) for slab in cross_1]
    state = attend(
        own,
        behind_1 + cross_1 + behind_1_sib + cross_1_sib,
        score_scale,
        jnp.stack([flag(1), flag(-1), flag(-1), flag(1)]),
        (max_0, total_0, sum_0),
    )
    behind_2_sib = [moved(slab, sibling) for slab in behind_2]
    cross_2_sib = [moved(slab, sibling) for slab in cross_2]
    state = attend(
        own, behind_2 + cross_2, score_scale, jnp.stack([flag(2), flag(-2)]), state
    )
    blended, own_log = attend(
        own,
        behind_2_sib + cross_2_sib,
        score_scale,
        jnp.stack([flag(-2), flag(2)]),
        state,
        last=True,
    )
    margin = pair_score - 0.5 * (own_log + moved(own_log, across_near))
    return (blended[None], margin)


def solution(mesh):
    placed = (P("dir", ("loop", "pb"), None), P())
    return jax.shard_map(
        shards,
        mesh=mesh,
        in_specs=placed,
        out_specs=(P("dir", ("loop", "pb"), None), P("dir", ("loop", "pb"))),
        check_vma=False,
    )
```

```python
import functools
import math

import jax
import jax.numpy as jnp
from jax import lax
from jax.experimental import pallas as pl
from jax.experimental.pallas import tpu as pltpu
from jax.sharding import PartitionSpec as P

sharpness = 3.0
AXES = ("dir", "loop", "pb")
PARTS = 1
VMEM = pl.BlockSpec(memory_space=pltpu.VMEM)
SMEM = pl.BlockSpec(memory_space=pltpu.SMEM)
ANY = pl.BlockSpec(memory_space=pl.ANY)


def moved(value, route):
    sides, blocks, slabs = (lax.axis_size(axis) for axis in AXES)
    pairs = []
    for side in range(sides):
        for block in range(blocks):
            for slab in range(slabs):
                half, core = divmod(slab, 2)
                side_to, block_to, half_to, core_to = route(side, block, half, core)
                target = (side_to * blocks + block_to % blocks) * slabs + half_to * 2 + core_to
                pairs.append(((side * blocks + block) * slabs + slab, target))
    return lax.ppermute(value, AXES, pairs)


def across_near(side, block, half, core):
    return 1 - side, block, half, core


def across_far(side, block, half, core):
    return 1 - side, block, 1 - half, core


def across_other(side, block, half, core):
    return 1 - side, block, half, 1 - core


def sibling(side, block, half, core):
    return side, block, half, 1 - core


def ahead(side, block, half, core):
    return side, block + (1 if core == 0 else -1), half, core


def behind(side, block, half, core):
    return side, block - (1 if core == 0 else -1), half, core


def attend_kernel(first, last, level, score_scale, *refs):
    refs = list(refs)

    def take(count):
        return [refs.pop(0) for _ in range(count)]

    if not first:
        (mask_ref,) = take(1)
    query_refs = take(2)
    state_in = [] if first else take(3)
    slab_refs = take(len(refs) - (7 if first else 10 if last else 6))
    if first:
        max_ref, total_ref, sum_ref, pair_ref = take(4)
    elif last:
        own_sum_ref, other_sum_ref, own_stat_ref, other_stat_ref = take(4)
        max_ref, total_ref, sum_ref = take(3)
    else:
        max_ref, total_ref, sum_ref = take(3)
    query_ref, key_ref, copy_sems = refs
    rows = query_ref.shape[0] // 2
    copies = []
    for sources, target in ((query_refs, query_ref), (slab_refs, key_ref)):
        begin = 0
        for source in sources:
            copy = pltpu.make_async_copy(
                source, target.at[pl.ds(begin, source.shape[0])], copy_sems.at[len(copies)]
            )
            copy.start()
            copies.append(copy)
            begin += source.shape[0]

    def absorb():
        keys = key_ref[...]
        for start in (rows, 0):
            here = pl.ds(start, rows)
            scores = (
                lax.dot_general(
                    query_ref[here, :], keys, (((1,), (1,)), ((), ())),
                    preferred_element_type=jnp.float32,
                )
                * score_scale
            )
            new_max = jnp.max(scores, axis=1, keepdims=True)
            if not first:
                new_max = jnp.maximum(state_in[0][here, :], new_max)
            weights = jnp.exp(scores - new_max)
            total = jnp.sum(weights, axis=1, keepdims=True)
            blended = jnp.dot(weights.astype(jnp.bfloat16), keys, preferred_element_type=jnp.float32)
            if not first:
                correction = jnp.exp(state_in[0][here, :] - new_max)
                total += state_in[1][here, :] * correction
                blended += state_in[2][here, :] * correction
            max_ref[here, :] = new_max
            total_ref[here, :] = total
            sum_ref[here, :] = blended

    for copy in copies:
        copy.wait()
    if first:
        absorb()
        pair_ref[...] = (
            jnp.sum(
                query_ref[:rows, :].astype(jnp.float32) * key_ref[:rows, :].astype(jnp.float32),
                axis=1,
                keepdims=True,
            )
            * score_scale
        ).T
    else:
        side, block = lax.axis_index("dir"), lax.axis_index("loop")
        blocks = mask_ref.shape[0]
        offset = jnp.where(lax.axis_index("pb") % 2 == 0, level, -level)
        target = lax.rem(block + offset + blocks, blocks)
        flag = jnp.where(side == 0, mask_ref[block, target], mask_ref[target, block])
        pl.when(flag > 0)(absorb)

        @pl.when(flag <= 0)
        def _():
            max_ref[...] = state_in[0][...]
            total_ref[...] = state_in[1][...]
            sum_ref[...] = state_in[2][...]

    if last:
        for index, (sum_out, stat_out) in enumerate(
            [(own_sum_ref, own_stat_ref), (other_sum_ref, other_stat_ref)]
        ):
            here = pl.ds(index * rows, rows)
            sum_out[...] = sum_ref[here, :]
            stat_out[0:1, :] = max_ref[here, :].T
            stat_out[1:2, :] = total_ref[here, :].T


def attend(queries, slabs, score_scale, level=0, mask=None, state=None, last=False):
    rows, width = queries[0].shape
    first = state is None
    keys = sum(slab.shape[0] for slab in slabs)
    held = [
        jax.ShapeDtypeStruct((2 * rows, 1), jnp.float32),
        jax.ShapeDtypeStruct((2 * rows, 1), jnp.float32),
        jax.ShapeDtypeStruct((2 * rows, width), jnp.float32),
    ]
    scratch = [
        pltpu.VMEM((2 * rows, width), jnp.bfloat16),
        pltpu.VMEM((keys, width), jnp.bfloat16),
        pltpu.SemaphoreType.DMA((len(slabs) + 2,)),
    ]
    if first:
        out = held + [jax.ShapeDtypeStruct((1, rows), jnp.float32)]
    elif last:
        out = [jax.ShapeDtypeStruct((rows, width), jnp.float32)] * 2
        out += [jax.ShapeDtypeStruct((2, rows), jnp.float32)] * 2
        scratch = [pltpu.VMEM(a.shape, a.dtype) for a in held] + scratch
    else:
        out = held
    in_specs = [ANY, ANY] if first else [SMEM, ANY, ANY, VMEM, VMEM, VMEM]
    operands = list(queries) if first else [mask] + list(queries) + list(state)
    return pl.pallas_call(
        functools.partial(attend_kernel, first, last, level, score_scale),
        out_shape=out,
        in_specs=in_specs + [ANY] * len(slabs),
        out_specs=[VMEM] * len(out),
        scratch_shapes=scratch,
        compiler_params=pltpu.CompilerParams(vmem_limit_bytes=24 * 2**20),
        cost_estimate=pl.CostEstimate(
            flops=8 * keys * rows * width,
            bytes_accessed=2 * (keys + 2 * rows) * width + 16 * rows * width,
            transcendentals=2 * keys * rows,
        ),
    )(*operands, *slabs)


def finish_kernel(
    sum_ref, sum_in_ref, stat_ref, stat_in_ref, far_stat_ref, far_stat_in_ref, pair_ref,
    blended_ref, margin_ref,
):
    def merged(here, there):
        top = jnp.maximum(here[0:1, :], there[0:1, :])
        left, right = jnp.exp(here[0:1, :] - top), jnp.exp(there[0:1, :] - top)
        total = here[1:2, :] * left + there[1:2, :] * right
        return left, right, total, top + jnp.log(total)

    left, right, total, own_log = merged(stat_ref[...], stat_in_ref[...])
    far_log = merged(far_stat_ref[...], far_stat_in_ref[...])[3]
    margin_ref[...] = pair_ref[...] - 0.5 * (own_log + far_log)
    blended_ref[...] = (
        sum_ref[...] * (left / total).T + sum_in_ref[...] * (right / total).T
    ).astype(jnp.bfloat16)


def finish(*operands):
    rows, width = operands[0].shape
    return pl.pallas_call(
        finish_kernel,
        out_shape=[
            jax.ShapeDtypeStruct((rows, width), jnp.bfloat16),
            jax.ShapeDtypeStruct((1, rows), jnp.float32),
        ],
        in_specs=[VMEM] * len(operands),
        out_specs=[VMEM] * 2,
        compiler_params=pltpu.CompilerParams(vmem_limit_bytes=20 * 2**20),
    )(*operands)


def shards(embeddings, block_mask):
    own = embeddings[0]
    score_scale = sharpness / math.sqrt(own.shape[1])
    rows = own.shape[0]
    part = rows // PARTS
    parts = [own[start : start + part] for start in range(0, rows, part)]

    ahead_1 = moved(own, ahead)
    near = [moved(piece, across_near) for piece in parts]
    far = [moved(piece, across_far) for piece in parts]
    queries = (own, moved(own, sibling))
    ahead_2 = moved(ahead_1, ahead)
    cross_1 = [moved(ahead_1, across_near), moved(ahead_1, across_far)]
    behind_1 = [moved(piece, behind) for piece in near + far]
    *state, pair_score = attend(queries, near + far, score_scale)
    ahead_2, state[0] = lax.optimization_barrier((ahead_2, state[0]))
    cross_2 = [moved(ahead_2, across_near), moved(ahead_2, across_far)]
    state = list(attend(queries, cross_1, score_scale, -1, block_mask, state))
    behind_2 = [moved(piece, behind) for piece in behind_1]
    state = attend(queries, behind_1, score_scale, 1, block_mask, state)
    state = attend(queries, cross_2, score_scale, -2, block_mask, state)
    own_sum, other_sum, own_stat, other_stat = attend(
        queries, behind_2, score_scale, 2, block_mask, state, last=True
    )
    blended, margin = finish(
        own_sum,
        moved(other_sum, sibling),
        own_stat,
        moved(other_stat, sibling),
        moved(own_stat, across_near),
        moved(other_stat, across_other),
        pair_score,
    )
    return (blended[None], margin)


def solution(mesh):
    placed = (P("dir", ("loop", "pb"), None), P())
    return jax.shard_map(
        shards,
        mesh=mesh,
        in_specs=placed,
        out_specs=(P("dir", ("loop", "pb"), None), P("dir", ("loop", "pb"))),
        check_vma=False,
    )
```

```python
import functools
import math

import jax
import jax.numpy as jnp
from jax import lax
from jax.experimental import pallas as pl
from jax.experimental.pallas import tpu as pltpu
from jax.sharding import PartitionSpec as P

sharpness = 3.0
AXES = ("dir", "loop", "pb")
LOG2_E = math.log2(math.e)
VMEM = pl.BlockSpec(memory_space=pltpu.VMEM)
SMEM = pl.BlockSpec(memory_space=pltpu.SMEM)


def moved(value, route):
    sides, blocks, slabs = (lax.axis_size(axis) for axis in AXES)
    pairs = []
    for side in range(sides):
        for block in range(blocks):
            for slab in range(slabs):
                half, core = divmod(slab, 2)
                side_to, block_to, half_to, core_to = route(side, block, half, core)
                target = (side_to * blocks + block_to % blocks) * slabs + half_to * 2 + core_to
                pairs.append(((side * blocks + block) * slabs + slab, target))
    return lax.ppermute(value, AXES, pairs)


def across_near(side, block, half, core):
    return 1 - side, block, half, core


def across_far(side, block, half, core):
    return 1 - side, block, 1 - half, core


def other_half(side, block, half, core):
    return side, block, 1 - half, core


def sibling(side, block, half, core):
    return side, block, half, 1 - core


def forward(side, block, half, core):
    return side, block + 1, half, core


def backward(side, block, half, core):
    return side, block - 1, half, core


def key_bias(mask_ref, offsets, rows):
    side, block = lax.axis_index("dir"), lax.axis_index("loop")
    blocks = mask_ref.shape[0]
    column = lax.broadcasted_iota(jnp.int32, (1, rows * len(offsets)), 1)
    bias = jnp.zeros(column.shape, jnp.float32)
    for index, offset in enumerate(offsets):
        target = lax.rem(block + offset + blocks, blocks)
        flag = jnp.where(side == 1, mask_ref[block, target], mask_ref[target, block])
        here = (column >= index * rows) & (column < (index + 1) * rows)
        bias = jnp.where(here & (flag <= 0), -jnp.inf, bias)
    return bias


def flash(query_ref, key_refs, score_scale, bias, state, out, begin, chunk, chunks):
    keys = jnp.concatenate([ref[...] for ref in key_refs], axis=0)
    heres = [pl.ds(begin + index * chunk, chunk) for index in range(chunks)]
    max_ref, total_ref, sum_ref = out

    def scored(here):
        scores = lax.dot_general(
            query_ref[here, :], keys, (((1,), (1,)), ((), ())), preferred_element_type=jnp.float32
        )
        return scores if bias is None else scores + bias

    ahead = scored(heres[0])
    for index, here in enumerate(heres):
        scores = ahead
        if index + 1 < chunks:
            ahead = scored(heres[index + 1])
        new_max = jnp.max(scores, axis=1, keepdims=True)
        if state:
            old_max = state[0][here, :]
            new_max = jnp.maximum(old_max, new_max)
        weights = jnp.exp2((scores - new_max) * (score_scale * LOG2_E))
        total = jnp.sum(weights, axis=1, keepdims=True)
        blended = jnp.dot(weights.astype(jnp.bfloat16), keys, preferred_element_type=jnp.float32)
        if state:
            correction = jnp.exp2((old_max - new_max) * (score_scale * LOG2_E))
            total += state[1][here, :] * correction
            blended += state[2][here, :] * correction
        max_ref[here, :] = new_max
        total_ref[here, :] = total
        sum_ref[here, :] = blended


def thirds_kernel(one_ref, two_ref, *pieces):
    rows = one_ref.shape[0]
    size = pieces[0].shape[0]
    pieces[0][...] = one_ref[:size, :]
    pieces[1][: rows - size, :] = one_ref[size:, :]
    pieces[1][rows - size :, :] = two_ref[: 2 * size - rows, :]
    pieces[2][...] = two_ref[2 * size - rows :, :]


def parts_of(rows):
    return rows - rows // 3, rows // 3


def first_kernel(
    score_scale, near_ref, far_ref, own_ref, sibling_ref,
    max_ref, total_ref, sum_ref, pair_ref, query_ref,
):
    rows = own_ref.shape[0]
    early, late = parts_of(rows)
    query_ref[:early, :] = near_ref[:early, :]
    query_ref[early : 2 * early, :] = far_ref[:early, :]
    query_ref[2 * early : 2 * early + late, :] = near_ref[early:, :]
    query_ref[2 * early + late :, :] = far_ref[early:, :]

    flash(
        query_ref, (own_ref, sibling_ref), score_scale, None, None,
        (max_ref, total_ref, sum_ref), 0, rows, 2,
    )
    pair_ref[...] = (
        jnp.sum(
            near_ref[...].astype(jnp.float32) * own_ref[...].astype(jnp.float32),
            axis=1,
            keepdims=True,
        )
        * score_scale
    ).T


def middle_kernel(score_scale, offsets, mask_ref, query_ref, *refs):
    state, key_refs, out = refs[:3], refs[3:-3], refs[-3:]
    rows = query_ref.shape[0] // 2
    bias = key_bias(mask_ref, offsets, rows)
    flash(query_ref, key_refs, score_scale, bias, state, out, 0, rows, 2)


def in_three(line):
    high = line.astype(jnp.bfloat16).astype(jnp.float32)
    middle = (line - high).astype(jnp.bfloat16).astype(jnp.float32)
    low = line - high - middle
    row = lax.broadcasted_iota(jnp.int32, (16, line.shape[1]), 0)
    tile = jnp.where(row == 0, high, jnp.where(row == 1, middle, jnp.where(row == 2, low, 0.0)))
    return tile.astype(jnp.bfloat16)


def of_three(tile):
    return jnp.sum(tile.astype(jnp.float32), axis=0, keepdims=True)


def last_kernel(score_scale, late, mask_ref, query_ref, *refs):
    state, key_refs, refs = refs[:3], refs[3:5], list(refs[5:])
    early_logs = [refs.pop(0), refs.pop(0)] if late else []
    near_ref, far_ref, near_log_ref, far_log_ref = refs[:4]
    out = refs[4:]
    rows = near_ref.shape[0] - (16 if late else 0)
    start = query_ref.shape[0] - 2 * rows if late else 0
    bias = key_bias(mask_ref, (-2, 2), key_refs[0].shape[0])
    chunks = 1 if late else 2
    flash(query_ref, key_refs, score_scale, bias, state, out, start, 2 * rows // chunks, chunks)
    max_ref, total_ref, sum_ref = out
    for index, (part_ref, log_ref) in enumerate(
        ((near_ref, near_log_ref), (far_ref, far_log_ref))
    ):
        these = pl.ds(start + index * rows, rows)
        total = total_ref[these, :]
        part_ref[:rows, :] = (sum_ref[these, :] / total).astype(jnp.bfloat16)
        log = (max_ref[these, :] * score_scale + jnp.log(total)).T
        if late:
            early = early_logs[index].shape[1]
            log_ref[:, :early] = early_logs[index][...]
            log_ref[:, early:] = log
            part_ref[rows:, :] = jnp.zeros((16, part_ref.shape[1]), jnp.bfloat16)
            part_ref[rows:, : early + rows] = in_three(log_ref[...])
        else:
            log_ref[...] = log


def call(kernel, out, operands, scratch=(), keys=0, query_rows=0, smem=False):
    width = max(operand.shape[1] for operand in operands)
    return pl.pallas_call(
        kernel,
        out_shape=out,
        in_specs=[SMEM if smem and index == 0 else VMEM for index in range(len(operands))],
        out_specs=[VMEM] * len(out),
        scratch_shapes=list(scratch),
        compiler_params=pltpu.CompilerParams(vmem_limit_bytes=24 * 2**20),
        cost_estimate=pl.CostEstimate(
            flops=4 * keys * query_rows * width,
            bytes_accessed=2 * (keys + query_rows) * width + 8 * query_rows * width,
            transcendentals=keys * query_rows,
        ),
    )(*operands)


def held(rows, width):
    return [
        jax.ShapeDtypeStruct((rows, 1), jnp.float32),
        jax.ShapeDtypeStruct((rows, 1), jnp.float32),
        jax.ShapeDtypeStruct((rows, width), jnp.float32),
    ]


def finish_kernel(
    here_log_ref, half_log_ref, pair_ref,
    near_early_ref, near_late_ref, far_early_ref, far_late_ref, blended_ref, margin_ref,
):
    def merged(one, two):
        top = jnp.maximum(one, two)
        return top + jnp.log(jnp.exp(one - top) + jnp.exp(two - top))

    rows, early = blended_ref.shape[0], near_early_ref.shape[0]
    late = rows - early
    near_log = of_three(near_late_ref[late:, :rows])
    far_log = of_three(far_late_ref[late:, :rows])
    own_log = merged(near_log, far_log)
    margin_ref[...] = pair_ref[...] - 0.5 * (
        own_log + merged(here_log_ref[...], half_log_ref[...])
    )
    near_share, far_share = jnp.exp(near_log - own_log).T, jnp.exp(far_log - own_log).T
    for here, count, near_ref, far_ref in (
        (slice(0, early), early, near_early_ref, far_early_ref),
        (slice(early, rows), late, near_late_ref, far_late_ref),
    ):
        blended_ref[here, :] = (
            near_ref[:count, :].astype(jnp.float32) * near_share[here, :]
            + far_ref[:count, :].astype(jnp.float32) * far_share[here, :]
        ).astype(jnp.bfloat16)


def after(value, *others):
    return lax.optimization_barrier((value, *others))[0]


def shards(embeddings, block_mask):
    own = embeddings[0]
    rows, width = own.shape
    early, late = parts_of(rows)
    score_scale = sharpness / math.sqrt(width)
    line = jax.ShapeDtypeStruct((1, rows), jnp.float32)

    near = moved(own, across_near)
    far = moved(own, across_far)
    before_1 = moved(own, forward)
    after_1 = moved(own, backward)
    own_sib = moved(own, sibling)

    before_2, after_2 = moved(before_1, forward), moved(after_1, backward)
    piece = jax.ShapeDtypeStruct((2 * rows // 3, width), own.dtype)
    ring_1 = call(thirds_kernel, [piece] * 3, [before_1, after_1])
    ring_1_sib = [moved(value, sibling) for value in ring_1]
    *state, pair_score, queries = call(
        functools.partial(first_kernel, score_scale),
        held(2 * rows, width) + [line, jax.ShapeDtypeStruct((2 * rows, width), jnp.bfloat16)],
        [near, far, own, own_sib],
    )
    state = call(
        functools.partial(middle_kernel, score_scale, (-1, 1, -1, 1)),
        held(2 * rows, width),
        [block_mask, queries, *state, before_1, after_1, *ring_1_sib],
        smem=True,
    )
    before_2, after_2, state = lax.optimization_barrier((before_2, after_2, state))
    before_2_sib, after_2_sib = moved(before_2, sibling), moved(after_2, sibling)
    state = call(
        functools.partial(middle_kernel, score_scale, (-2, 2)),
        held(2 * rows, width),
        [block_mask, queries, *state, before_2, after_2],
        keys=2 * rows, query_rows=2 * rows, smem=True,
    )
    logs, sent = [], []
    for size in (early, late):
        near_part, far_part, *logs = call(
            functools.partial(last_kernel, score_scale, bool(sent)),
            [jax.ShapeDtypeStruct((size + (16 if sent else 0), width), jnp.bfloat16)] * 2
            + [jax.ShapeDtypeStruct((1, rows if sent else size), jnp.float32)] * 2,
            [block_mask, queries, *state, before_2_sib, after_2_sib, *logs],
            scratch=[pltpu.VMEM(a.shape, a.dtype) for a in held(2 * rows, width)],
            keys=2 * rows, query_rows=2 * size, smem=True,
        )
        sent.append((moved(near_part, across_near), moved(far_part, across_far)))
    near_log, far_log = logs
    blended, margin = call(
        finish_kernel,
        [jax.ShapeDtypeStruct((rows, width), jnp.bfloat16), line],
        [
            near_log,
            moved(far_log, other_half),
            pair_score,
            sent[0][0], sent[1][0], sent[0][1], sent[1][1],
        ],
    )
    return (blended[None], margin)


def solution(mesh):
    placed = (P("dir", ("loop", "pb"), None), P())
    return jax.shard_map(
        shards,
        mesh=mesh,
        in_specs=placed,
        out_specs=(P("dir", ("loop", "pb"), None), P("dir", ("loop", "pb"))),
        check_vma=False,
    )
```

```python
import functools
import math

import jax
import jax.numpy as jnp
from jax import lax
from jax.experimental import pallas as pl
from jax.experimental.pallas import tpu as pltpu
from jax.sharding import PartitionSpec as P

sharpness = 3.0
AXES = ("dir", "loop", "pb")
LOG2_E = math.log2(math.e)
VMEM = pl.BlockSpec(memory_space=pltpu.VMEM)
SMEM = pl.BlockSpec(memory_space=pltpu.SMEM)
ANY = pl.BlockSpec(memory_space=pl.ANY)


def moved(value, route):
    sides, blocks, slabs = (lax.axis_size(axis) for axis in AXES)
    pairs = []
    for side in range(sides):
        for block in range(blocks):
            for slab in range(slabs):
                half, core = divmod(slab, 2)
                side_to, block_to, half_to, core_to = route(side, block, half, core)
                target = (side_to * blocks + block_to % blocks) * slabs + half_to * 2 + core_to
                pairs.append(((side * blocks + block) * slabs + slab, target))
    return lax.ppermute(value, AXES, pairs)


def across_near(side, block, half, core):
    return 1 - side, block, half, core


def across_far(side, block, half, core):
    return 1 - side, block, 1 - half, core


def other_half(side, block, half, core):
    return side, block, 1 - half, core


def sibling(side, block, half, core):
    return side, block, half, 1 - core


def onward(side, block, half, core):
    return side, block + (1 if core == 0 else -1), half, core


def key_bias(mask_ref, offsets, rows):
    side, block = lax.axis_index("dir"), lax.axis_index("loop")
    sign = jnp.where(lax.axis_index("pb") % 2 == 0, -1, 1)
    blocks = mask_ref.shape[0]
    column = lax.broadcasted_iota(jnp.int32, (1, rows * len(offsets)), 1)
    bias = jnp.zeros(column.shape, jnp.float32)
    for index, offset in enumerate(offsets):
        target = lax.rem(block + offset * sign + blocks, blocks)
        flag = jnp.where(side == 1, mask_ref[block, target], mask_ref[target, block])
        here = (column >= index * rows) & (column < (index + 1) * rows)
        bias = jnp.where(here & (flag <= 0), -jnp.inf, bias)
    return bias


def flash(query_ref, key_refs, score_scale, bias, state, out, begin, chunk, chunks):
    keys = jnp.concatenate([ref[...] for ref in key_refs], axis=0)
    heres = [pl.ds(begin + index * chunk, chunk) for index in range(chunks)]
    max_ref, total_ref, sum_ref = out

    def scored(here):
        scores = lax.dot_general(
            query_ref[here, :], keys, (((1,), (1,)), ((), ())), preferred_element_type=jnp.float32
        )
        return scores if bias is None else scores + bias

    ahead = scored(heres[0])
    for index, here in enumerate(heres):
        scores = ahead
        if index + 1 < chunks:
            ahead = scored(heres[index + 1])
        new_max = jnp.max(scores, axis=1, keepdims=True)
        if state:
            old_max = state[0][here, :]
            new_max = jnp.maximum(old_max, new_max)
        weights = jnp.exp2((scores - new_max) * (score_scale * LOG2_E))
        total = jnp.sum(weights, axis=1, keepdims=True)
        blended = jnp.dot(weights.astype(jnp.bfloat16), keys, preferred_element_type=jnp.float32)
        if state:
            correction = jnp.exp2((old_max - new_max) * (score_scale * LOG2_E))
            total += state[1][here, :] * correction
            blended += state[2][here, :] * correction
        max_ref[here, :] = new_max
        total_ref[here, :] = total
        sum_ref[here, :] = blended


def parts_of(rows):
    return rows - rows // 3, rows // 3


def first_kernel(
    score_scale, near_ref, far_ref, own_ref, sibling_ref,
    max_ref, total_ref, sum_ref, query_ref, held_ref, copy_sem,
):
    rows = own_ref.shape[0]
    early, late = parts_of(rows)
    copy = pltpu.make_async_copy(own_ref, held_ref, copy_sem)
    copy.start()
    query_ref[:early, :] = near_ref[:early, :]
    query_ref[early : 2 * early, :] = far_ref[:early, :]
    query_ref[2 * early : 2 * early + late, :] = near_ref[early:, :]
    query_ref[2 * early + late :, :] = far_ref[early:, :]
    copy.wait()
    flash(
        query_ref, (held_ref, sibling_ref), score_scale, None, None,
        (max_ref, total_ref, sum_ref), 0, rows, 2,
    )


def pair_kernel(score_scale, near_ref, own_ref, pair_ref):
    pair_ref[...] = (
        jnp.sum(
            near_ref[...].astype(jnp.float32) * own_ref[...].astype(jnp.float32),
            axis=1,
            keepdims=True,
        )
        * score_scale
    ).T


def middle_kernel(score_scale, offsets, mask_ref, query_ref, *refs):
    state, key_refs, out = refs[:3], refs[3:-3], refs[-3:]
    rows = query_ref.shape[0] // 2
    bias = key_bias(mask_ref, offsets, rows)
    flash(query_ref, key_refs, score_scale, bias, state, out, 0, rows, 2)


def in_three(line):
    high = line.astype(jnp.bfloat16).astype(jnp.float32)
    middle = (line - high).astype(jnp.bfloat16).astype(jnp.float32)
    low = line - high - middle
    row = lax.broadcasted_iota(jnp.int32, (16, line.shape[1]), 0)
    tile = jnp.where(row == 0, high, jnp.where(row == 1, middle, jnp.where(row == 2, low, 0.0)))
    return tile.astype(jnp.bfloat16)


def of_three(tile):
    return jnp.sum(tile.astype(jnp.float32), axis=0, keepdims=True)


def last_kernel(score_scale, late, mask_ref, query_ref, *refs):
    state, key_refs, refs = refs[:3], refs[3:5], list(refs[5:])
    early_logs = [refs.pop(0), refs.pop(0)] if late else []
    near_ref, far_ref, near_log_ref, far_log_ref = refs[:4]
    out = refs[4:]
    rows = near_ref.shape[0] - (16 if late else 0)
    start = query_ref.shape[0] - 2 * rows if late else 0
    bias = key_bias(mask_ref, (2, -2), key_refs[0].shape[0])
    chunks = 1 if late else 2
    flash(query_ref, key_refs, score_scale, bias, state, out, start, 2 * rows // chunks, chunks)
    max_ref, total_ref, sum_ref = out
    for index, (part_ref, log_ref) in enumerate(
        ((near_ref, near_log_ref), (far_ref, far_log_ref))
    ):
        these = pl.ds(start + index * rows, rows)
        total = total_ref[these, :]
        part_ref[:rows, :] = (sum_ref[these, :] / total).astype(jnp.bfloat16)
        log = (max_ref[these, :] * score_scale + jnp.log(total)).T
        if late:
            early = early_logs[index].shape[1]
            log_ref[:, :early] = early_logs[index][...]
            log_ref[:, early:] = log
            part_ref[rows:, :] = jnp.zeros((16, part_ref.shape[1]), jnp.bfloat16)
            part_ref[rows:, : early + rows] = in_three(log_ref[...])
        else:
            log_ref[...] = log


def call(kernel, out, operands, scratch=(), keys=0, query_rows=0, smem=False, left=()):
    width = max(operand.shape[1] for operand in operands)
    return pl.pallas_call(
        kernel,
        out_shape=out,
        in_specs=[
            SMEM if smem and index == 0 else ANY if index in left else VMEM
            for index in range(len(operands))
        ],
        out_specs=[VMEM] * len(out),
        scratch_shapes=list(scratch),
        compiler_params=pltpu.CompilerParams(vmem_limit_bytes=24 * 2**20),
        cost_estimate=pl.CostEstimate(
            flops=4 * keys * query_rows * width,
            bytes_accessed=2 * (keys + query_rows) * width + 8 * query_rows * width,
            transcendentals=keys * query_rows,
        ),
    )(*operands)


def held(rows, width):
    return [
        jax.ShapeDtypeStruct((rows, 1), jnp.float32),
        jax.ShapeDtypeStruct((rows, 1), jnp.float32),
        jax.ShapeDtypeStruct((rows, width), jnp.float32),
    ]


def finish_kernel(
    here_log_ref, half_log_ref, pair_ref,
    near_early_ref, near_late_ref, far_early_ref, far_late_ref, blended_ref, margin_ref,
):
    def merged(one, two):
        top = jnp.maximum(one, two)
        return top + jnp.log(jnp.exp(one - top) + jnp.exp(two - top))

    rows, early = blended_ref.shape[0], near_early_ref.shape[0]
    late = rows - early
    near_log = of_three(near_late_ref[late:, :rows])
    far_log = of_three(far_late_ref[late:, :rows])
    own_log = merged(near_log, far_log)
    margin_ref[...] = pair_ref[...] - 0.5 * (
        own_log + merged(here_log_ref[...], half_log_ref[...])
    )
    near_share, far_share = jnp.exp(near_log - own_log).T, jnp.exp(far_log - own_log).T
    for here, count, near_ref, far_ref in (
        (slice(0, early), early, near_early_ref, far_early_ref),
        (slice(early, rows), late, near_late_ref, far_late_ref),
    ):
        blended_ref[here, :] = (
            near_ref[:count, :].astype(jnp.float32) * near_share[here, :]
            + far_ref[:count, :].astype(jnp.float32) * far_share[here, :]
        ).astype(jnp.bfloat16)


def after(value, *others):
    return lax.optimization_barrier((value, *others))[0]


def shards(embeddings, block_mask):
    own = embeddings[0]
    rows, width = own.shape
    early, late = parts_of(rows)
    score_scale = sharpness / math.sqrt(width)
    line = jax.ShapeDtypeStruct((1, rows), jnp.float32)

    near = moved(own, across_near)
    far = moved(own, across_far)
    own_sib = moved(own, sibling)
    first_1, second_1 = moved(own, onward), moved(own_sib, onward)
    first_2, second_2 = moved(first_1, onward), moved(second_1, onward)
    first_1_sib, second_1_sib = moved(first_1, sibling), moved(second_1, sibling)
    *state, queries = call(
        functools.partial(first_kernel, score_scale),
        held(2 * rows, width) + [jax.ShapeDtypeStruct((2 * rows, width), jnp.bfloat16)],
        [near, far, own, own_sib],
        scratch=[pltpu.VMEM(own.shape, own.dtype), pltpu.SemaphoreType.DMA(())],
        left=(2,),
    )
    first_2, state = lax.optimization_barrier((first_2, state))
    first_2_sib = moved(first_2, sibling)
    state = call(
        functools.partial(middle_kernel, score_scale, (1, 1, -1, -1)),
        held(2 * rows, width),
        [block_mask, queries, *state, first_1, second_1, first_1_sib, second_1_sib],
        smem=True,
    )
    second_2, state = lax.optimization_barrier((second_2, state))
    second_2_sib = moved(second_2, sibling)
    state = call(
        functools.partial(middle_kernel, score_scale, (2, -2)),
        held(2 * rows, width),
        [block_mask, queries, *state, first_2, first_2_sib],
        keys=2 * rows, query_rows=2 * rows, smem=True,
    )
    logs, sent = [], []
    for size in (early, late):
        near_part, far_part, *logs = call(
            functools.partial(last_kernel, score_scale, bool(sent)),
            [jax.ShapeDtypeStruct((size + (16 if sent else 0), width), jnp.bfloat16)] * 2
            + [jax.ShapeDtypeStruct((1, rows if sent else size), jnp.float32)] * 2,
            [block_mask, queries, *state, second_2, second_2_sib, *logs],
            scratch=[pltpu.VMEM(a.shape, a.dtype) for a in held(2 * rows, width)],
            keys=2 * rows, query_rows=2 * size, smem=True,
        )
        sent.append((moved(near_part, across_near), moved(far_part, across_far)))
    near_log, far_log = logs
    pair_score = call(
        functools.partial(pair_kernel, score_scale), [line], [after(near, near_log), own]
    )[0]
    blended, margin = call(
        finish_kernel,
        [jax.ShapeDtypeStruct((rows, width), jnp.bfloat16), line],
        [
            near_log,
            moved(far_log, other_half),
            pair_score,
            sent[0][0], sent[1][0], sent[0][1], sent[1][1],
        ],
    )
    return (blended[None], margin)


def solution(mesh):
    placed = (P("dir", ("loop", "pb"), None), P())
    return jax.shard_map(
        shards,
        mesh=mesh,
        in_specs=placed,
        out_specs=(P("dir", ("loop", "pb"), None), P("dir", ("loop", "pb"))),
        check_vma=False,
    )
```

```python
import functools
import math

import jax
import jax.numpy as jnp
from jax import lax
from jax.experimental import pallas as pl
from jax.experimental.pallas import tpu as pltpu
from jax.sharding import PartitionSpec as P

sharpness = 3.0
AXES = ("dir", "loop", "pb")
LOG2_E = math.log2(math.e)
VMEM = pl.BlockSpec(memory_space=pltpu.VMEM)
SMEM = pl.BlockSpec(memory_space=pltpu.SMEM)
ANY = pl.BlockSpec(memory_space=pl.ANY)


def moved(value, route):
    sides, blocks, slabs = (lax.axis_size(axis) for axis in AXES)
    pairs = []
    for side in range(sides):
        for block in range(blocks):
            for slab in range(slabs):
                half, core = divmod(slab, 2)
                side_to, block_to, half_to, core_to = route(side, block, half, core)
                target = (side_to * blocks + block_to % blocks) * slabs + half_to * 2 + core_to
                pairs.append(((side * blocks + block) * slabs + slab, target))
    return lax.ppermute(value, AXES, pairs)


def across_near(side, block, half, core):
    return 1 - side, block, half, core


def across_far(side, block, half, core):
    return 1 - side, block, 1 - half, core


def other_half(side, block, half, core):
    return side, block, 1 - half, core


def sibling(side, block, half, core):
    return side, block, half, 1 - core


def onward(side, block, half, core):
    return side, block + (1 if core == 0 else -1), half, core


def key_bias(mask_ref, offsets, rows):
    side, block = lax.axis_index("dir"), lax.axis_index("loop")
    sign = jnp.where(lax.axis_index("pb") % 2 == 0, -1, 1)
    blocks = mask_ref.shape[0]
    column = lax.broadcasted_iota(jnp.int32, (1, rows * len(offsets)), 1)
    bias = jnp.zeros(column.shape, jnp.float32)
    for index, offset in enumerate(offsets):
        target = lax.rem(block + offset * sign + blocks, blocks)
        flag = jnp.where(side == 1, mask_ref[block, target], mask_ref[target, block])
        here = (column >= index * rows) & (column < (index + 1) * rows)
        bias = jnp.where(here & (flag <= 0), -jnp.inf, bias)
    return bias


def flash(query_ref, key_refs, score_scale, bias, state, out, begin, chunk, chunks):
    keys = jnp.concatenate([ref[...] for ref in key_refs], axis=0)
    heres = [pl.ds(begin + index * chunk, chunk) for index in range(chunks)]
    max_ref, total_ref, sum_ref = out

    def scored(here):
        scores = lax.dot_general(
            query_ref[here, :], keys, (((1,), (1,)), ((), ())), preferred_element_type=jnp.float32
        )
        return scores if bias is None else scores + bias

    ahead = scored(heres[0])
    for index, here in enumerate(heres):
        scores = ahead
        if index + 1 < chunks:
            ahead = scored(heres[index + 1])
        new_max = jnp.max(scores, axis=1, keepdims=True)
        if state:
            old_max = state[0][here, :]
            new_max = jnp.maximum(old_max, new_max)
        weights = jnp.exp2((scores - new_max) * (score_scale * LOG2_E))
        total = jnp.sum(weights, axis=1, keepdims=True)
        blended = jnp.dot(weights.astype(jnp.bfloat16), keys, preferred_element_type=jnp.float32)
        if state:
            correction = jnp.exp2((old_max - new_max) * (score_scale * LOG2_E))
            total += state[1][here, :] * correction
            blended += state[2][here, :] * correction
        max_ref[here, :] = new_max
        total_ref[here, :] = total
        sum_ref[here, :] = blended


def parts_of(rows):
    return rows - rows // 3, rows // 3


def first_kernel(
    score_scale, near_ref, far_ref, own_ref, sibling_ref,
    max_ref, total_ref, sum_ref, query_ref, held_ref, copy_sem,
):
    rows = own_ref.shape[0]
    early, late = parts_of(rows)
    copy = pltpu.make_async_copy(own_ref, held_ref, copy_sem)
    copy.start()
    query_ref[:early, :] = near_ref[:early, :]
    query_ref[early : 2 * early, :] = far_ref[:early, :]
    query_ref[2 * early : 2 * early + late, :] = near_ref[early:, :]
    query_ref[2 * early + late :, :] = far_ref[early:, :]
    copy.wait()
    flash(
        query_ref, (held_ref, sibling_ref), score_scale, None, None,
        (max_ref, total_ref, sum_ref), 0, rows, 2,
    )


def pair_kernel(score_scale, near_ref, own_ref, pair_ref):
    pair_ref[...] = (
        jnp.sum(
            near_ref[...].astype(jnp.float32) * own_ref[...].astype(jnp.float32),
            axis=1,
            keepdims=True,
        )
        * score_scale
    ).T


def middle_kernel(score_scale, offsets, mask_ref, query_ref, *refs):
    state, key_refs, out = refs[:3], refs[3:-3], refs[-3:]
    bias = key_bias(mask_ref, offsets, query_ref.shape[0] // 2)
    flash(query_ref, key_refs, score_scale, bias, state, out, 0, out[0].shape[0] // 2, 2)


def in_three(line):
    high = line.astype(jnp.bfloat16).astype(jnp.float32)
    middle = (line - high).astype(jnp.bfloat16).astype(jnp.float32)
    low = line - high - middle
    row = lax.broadcasted_iota(jnp.int32, (16, line.shape[1]), 0)
    tile = jnp.where(row == 0, high, jnp.where(row == 1, middle, jnp.where(row == 2, low, 0.0)))
    return tile.astype(jnp.bfloat16)


def of_three(tile):
    return jnp.sum(tile.astype(jnp.float32), axis=0, keepdims=True)


def last_kernel(score_scale, late, offsets, mask_ref, query_ref, *refs):
    count = len(offsets)
    state, key_refs, refs = refs[:3], refs[3 : 3 + count], list(refs[3 + count :])
    early_logs = [refs.pop(0), refs.pop(0)] if late else []
    near_ref, far_ref, near_log_ref, far_log_ref = refs[:4]
    out = refs[4:]
    rows = near_ref.shape[0] - (16 if late else 0)
    start = query_ref.shape[0] - 2 * rows if late else 0
    bias = key_bias(mask_ref, offsets, key_refs[0].shape[0])
    chunks = 1 if late else 2
    flash(query_ref, key_refs, score_scale, bias, state, out, start, 2 * rows // chunks, chunks)
    max_ref, total_ref, sum_ref = out
    for index, (part_ref, log_ref) in enumerate(
        ((near_ref, near_log_ref), (far_ref, far_log_ref))
    ):
        these = pl.ds(start + index * rows, rows)
        total = total_ref[these, :]
        part_ref[:rows, :] = (sum_ref[these, :] / total).astype(jnp.bfloat16)
        log = (max_ref[these, :] * score_scale + jnp.log(total)).T
        if late:
            early = early_logs[index].shape[1]
            log_ref[:, :early] = early_logs[index][...]
            log_ref[:, early:] = log
            part_ref[rows:, :] = jnp.zeros((16, part_ref.shape[1]), jnp.bfloat16)
            part_ref[rows:, : early + rows] = in_three(log_ref[...])
        else:
            log_ref[...] = log


def call(kernel, out, operands, scratch=(), keys=0, query_rows=0, smem=False, left=()):
    width = max(operand.shape[1] for operand in operands)
    return pl.pallas_call(
        kernel,
        out_shape=out,
        in_specs=[
            SMEM if smem and index == 0 else ANY if index in left else VMEM
            for index in range(len(operands))
        ],
        out_specs=[VMEM] * len(out),
        scratch_shapes=list(scratch),
        compiler_params=pltpu.CompilerParams(vmem_limit_bytes=24 * 2**20),
        cost_estimate=pl.CostEstimate(
            flops=4 * keys * query_rows * width,
            bytes_accessed=2 * (keys + query_rows) * width + 8 * query_rows * width,
            transcendentals=keys * query_rows,
        ),
    )(*operands)


def held(rows, width):
    return [
        jax.ShapeDtypeStruct((rows, 1), jnp.float32),
        jax.ShapeDtypeStruct((rows, 1), jnp.float32),
        jax.ShapeDtypeStruct((rows, width), jnp.float32),
    ]


def finish_kernel(
    here_log_ref, half_log_ref, pair_ref,
    near_early_ref, near_late_ref, far_early_ref, far_late_ref, blended_ref, margin_ref,
):
    def merged(one, two):
        top = jnp.maximum(one, two)
        return top + jnp.log(jnp.exp(one - top) + jnp.exp(two - top))

    rows, early = blended_ref.shape[0], near_early_ref.shape[0]
    late = rows - early
    near_log = of_three(near_late_ref[late:, :rows])
    far_log = of_three(far_late_ref[late:, :rows])
    own_log = merged(near_log, far_log)
    margin_ref[...] = pair_ref[...] - 0.5 * (
        own_log + merged(here_log_ref[...], half_log_ref[...])
    )
    near_share, far_share = jnp.exp(near_log - own_log).T, jnp.exp(far_log - own_log).T
    for here, count, near_ref, far_ref in (
        (slice(0, early), early, near_early_ref, far_early_ref),
        (slice(early, rows), late, near_late_ref, far_late_ref),
    ):
        blended_ref[here, :] = (
            near_ref[:count, :].astype(jnp.float32) * near_share[here, :]
            + far_ref[:count, :].astype(jnp.float32) * far_share[here, :]
        ).astype(jnp.bfloat16)


def after(value, *others):
    return lax.optimization_barrier((value, *others))[0]


def shards(embeddings, block_mask):
    own = embeddings[0]
    rows, width = own.shape
    early, late = parts_of(rows)
    score_scale = sharpness / math.sqrt(width)
    line = jax.ShapeDtypeStruct((1, rows), jnp.float32)

    near = moved(own, across_near)
    far = moved(own, across_far)
    own_sib = moved(own, sibling)
    first_1, second_1 = moved(own, onward), moved(own_sib, onward)
    first_2, second_2 = moved(first_1, onward), moved(second_1, onward)
    first_1_sib, second_1_sib = moved(after(first_1, near), sibling), moved(after(second_1, near), sibling)
    *state, queries = call(
        functools.partial(first_kernel, score_scale),
        held(2 * rows, width) + [jax.ShapeDtypeStruct((2 * rows, width), jnp.bfloat16)],
        [near, far, own, own_sib],
        scratch=[pltpu.VMEM(own.shape, own.dtype), pltpu.SemaphoreType.DMA(())],
        left=(2,),
    )
    first_2, state = lax.optimization_barrier((first_2, state))
    first_2_sib = moved(first_2, sibling)
    state = call(
        functools.partial(middle_kernel, score_scale, (1, 1, -1, -1)),
        held(2 * rows, width),
        [block_mask, queries, *state, first_1, second_1, first_1_sib, second_1_sib],
        smem=True,
    )
    second_2, state = lax.optimization_barrier((second_2, state))
    second_2_sib = moved(second_2, sibling)
    ring_2 = [first_2, first_2_sib, second_2, second_2_sib]
    early_state = call(
        functools.partial(middle_kernel, score_scale, (2, -2)),
        held(2 * early, width),
        [block_mask, queries, *state, *ring_2[:2]],
        keys=2 * rows, query_rows=2 * early, smem=True,
    )
    logs, sent = [], []
    for size, offsets, keys, source in (
        (early, (2, -2), ring_2[2:], early_state),
        (late, (2, -2, 2, -2), ring_2, state),
    ):
        near_part, far_part, *logs = call(
            functools.partial(last_kernel, score_scale, bool(sent), offsets),
            [jax.ShapeDtypeStruct((size + (16 if sent else 0), width), jnp.bfloat16)] * 2
            + [jax.ShapeDtypeStruct((1, rows if sent else size), jnp.float32)] * 2,
            [block_mask, queries, *source, *keys, *logs],
            scratch=[pltpu.VMEM(a.shape, a.dtype) for a in held(2 * rows, width)],
            keys=len(keys) * rows, query_rows=2 * size, smem=True,
        )
        sent.append((moved(near_part, across_near), moved(far_part, across_far)))
    near_log, far_log = logs
    pair_score = call(
        functools.partial(pair_kernel, score_scale), [line], [after(near, near_log), own]
    )[0]
    blended, margin = call(
        finish_kernel,
        [jax.ShapeDtypeStruct((rows, width), jnp.bfloat16), line],
        [
            near_log,
            moved(far_log, other_half),
            pair_score,
            sent[0][0], sent[1][0], sent[0][1], sent[1][1],
        ],
    )
    return (blended[None], margin)


def solution(mesh):
    placed = (P("dir", ("loop", "pb"), None), P())
    return jax.shard_map(
        shards,
        mesh=mesh,
        in_specs=placed,
        out_specs=(P("dir", ("loop", "pb"), None), P("dir", ("loop", "pb"))),
        check_vma=False,
    )
```

```python
import functools
import math

import jax
import jax.numpy as jnp
from jax import lax
from jax.experimental import pallas as pl
from jax.experimental.pallas import tpu as pltpu
from jax.sharding import PartitionSpec as P

sharpness = 3.0
AXES = ("dir", "loop", "pb")
LOG2_E = math.log2(math.e)
VMEM = pl.BlockSpec(memory_space=pltpu.VMEM)
SMEM = pl.BlockSpec(memory_space=pltpu.SMEM)
ANY = pl.BlockSpec(memory_space=pl.ANY)


def moved(value, route):
    sides, blocks, slabs = (lax.axis_size(axis) for axis in AXES)
    pairs = []
    for side in range(sides):
        for block in range(blocks):
            for slab in range(slabs):
                half, core = divmod(slab, 2)
                side_to, block_to, half_to, core_to = route(side, block, half, core)
                target = (side_to * blocks + block_to % blocks) * slabs + half_to * 2 + core_to
                pairs.append(((side * blocks + block) * slabs + slab, target))
    return lax.ppermute(value, AXES, pairs)


def across_near(side, block, half, core):
    return 1 - side, block, half, core


def across_far(side, block, half, core):
    return 1 - side, block, 1 - half, core


def other_half(side, block, half, core):
    return side, block, 1 - half, core


def sibling(side, block, half, core):
    return side, block, half, 1 - core


def onward(side, block, half, core):
    return side, block + (1 if core == 0 else -1), half, core


def key_bias(mask_ref, offsets, rows):
    side, block = lax.axis_index("dir"), lax.axis_index("loop")
    sign = jnp.where(lax.axis_index("pb") % 2 == 0, -1, 1)
    blocks = mask_ref.shape[0]
    column = lax.broadcasted_iota(jnp.int32, (1, rows * len(offsets)), 1)
    bias = jnp.zeros(column.shape, jnp.float32)
    for index, offset in enumerate(offsets):
        target = lax.rem(block + offset * sign + blocks, blocks)
        flag = jnp.where(side == 1, mask_ref[block, target], mask_ref[target, block])
        here = (column >= index * rows) & (column < (index + 1) * rows)
        bias = jnp.where(here & (flag <= 0), -jnp.inf, bias)
    return bias


def flash(query_ref, key_refs, score_scale, bias, state, out, begin, chunk, chunks):
    keys = jnp.concatenate([ref[...] for ref in key_refs], axis=0)
    heres = [pl.ds(begin + index * chunk, chunk) for index in range(chunks)]
    max_ref, total_ref, sum_ref = out

    def scored(here):
        scores = lax.dot_general(
            query_ref[here, :], keys, (((1,), (1,)), ((), ())), preferred_element_type=jnp.float32
        )
        return scores if bias is None else scores + bias

    ahead = scored(heres[0])
    for index, here in enumerate(heres):
        scores = ahead
        if index + 1 < chunks:
            ahead = scored(heres[index + 1])
        new_max = jnp.max(scores, axis=1, keepdims=True)
        if state:
            old_max = state[0][here, :]
            new_max = jnp.maximum(old_max, new_max)
        weights = jnp.exp2((scores - new_max) * (score_scale * LOG2_E))
        total = jnp.sum(weights, axis=1, keepdims=True)
        blended = jnp.dot(weights.astype(jnp.bfloat16), keys, preferred_element_type=jnp.float32)
        if state:
            correction = jnp.exp2((old_max - new_max) * (score_scale * LOG2_E))
            total += state[1][here, :] * correction
            blended += state[2][here, :] * correction
        max_ref[here, :] = new_max
        total_ref[here, :] = total
        sum_ref[here, :] = blended


def parts_of(rows):
    return rows - rows // 3, rows // 3


def first_kernel(
    score_scale, near_ref, far_ref, own_ref, sibling_ref,
    max_ref, total_ref, sum_ref, query_ref, held_ref, copy_sem,
):
    rows = own_ref.shape[0]
    early, late = parts_of(rows)
    copy = pltpu.make_async_copy(own_ref, held_ref, copy_sem)
    copy.start()
    query_ref[:early, :] = near_ref[:early, :]
    query_ref[early : 2 * early, :] = far_ref[:early, :]
    query_ref[2 * early : 2 * early + late, :] = near_ref[early:, :]
    query_ref[2 * early + late :, :] = far_ref[early:, :]
    copy.wait()
    flash(
        query_ref, (held_ref, sibling_ref), score_scale, None, None,
        (max_ref, total_ref, sum_ref), 0, rows, 2,
    )


def pair_kernel(score_scale, near_ref, own_ref, pair_ref):
    pair_ref[...] = (
        jnp.sum(
            near_ref[...].astype(jnp.float32) * own_ref[...].astype(jnp.float32),
            axis=1,
            keepdims=True,
        )
        * score_scale
    ).T


def middle_kernel(score_scale, offsets, mask_ref, query_ref, *refs):
    state, key_refs, out = refs[:3], refs[3:-3], refs[-3:]
    bias = key_bias(mask_ref, offsets, query_ref.shape[0] // 2)
    flash(query_ref, key_refs, score_scale, bias, state, out, 0, out[0].shape[0] // 2, 2)


def in_threes(lines):
    row = lax.broadcasted_iota(jnp.int32, (16, lines.shape[1]), 0)
    tile = jnp.zeros(row.shape, jnp.float32)
    for index in range(lines.shape[0]):
        line = lines[index : index + 1, :]
        high = line.astype(jnp.bfloat16).astype(jnp.float32)
        middle = (line - high).astype(jnp.bfloat16).astype(jnp.float32)
        for place, piece in enumerate((high, middle, line - high - middle)):
            tile = jnp.where(row == 3 * index + place, piece, tile)
    return tile.astype(jnp.bfloat16)


def of_threes(tile, index):
    high, middle, low = (
        tile[3 * index + place : 3 * index + place + 1, :].astype(jnp.float32)
        for place in range(3)
    )
    return low + middle + high


def last_kernel(score_scale, late, offsets, mask_ref, query_ref, *refs):
    count = len(offsets)
    state, key_refs, refs = refs[:3], refs[3 : 3 + count], list(refs[3 + count :])
    early_stats = [refs.pop(0), refs.pop(0)] if late else []
    near_ref, far_ref, near_stat_ref, far_stat_ref = refs[:4]
    out = refs[4:]
    rows = near_ref.shape[0] - (16 if late else 0)
    start = query_ref.shape[0] - 2 * rows if late else 0
    bias = key_bias(mask_ref, offsets, key_refs[0].shape[0])
    chunks = 1 if late else 2
    flash(query_ref, key_refs, score_scale, bias, state, out, start, 2 * rows // chunks, chunks)
    max_ref, total_ref, sum_ref = out
    for index, (part_ref, stat_ref) in enumerate(
        ((near_ref, near_stat_ref), (far_ref, far_stat_ref))
    ):
        these = pl.ds(start + index * rows, rows)
        total = total_ref[these, :]
        part_ref[:rows, :] = (sum_ref[these, :] / total).astype(jnp.bfloat16)
        early = early_stats[index].shape[1] if late else 0
        stat_ref[0:1, early:] = max_ref[these, :].T
        stat_ref[1:2, early:] = total.T
        if late:
            stat_ref[:, :early] = early_stats[index][...]
            part_ref[rows:, :] = jnp.zeros((16, part_ref.shape[1]), jnp.bfloat16)
            part_ref[rows:, : early + rows] = in_threes(stat_ref[...])


def call(kernel, out, operands, scratch=(), keys=0, query_rows=0, smem=False, left=()):
    width = max(operand.shape[1] for operand in operands)
    return pl.pallas_call(
        kernel,
        out_shape=out,
        in_specs=[
            SMEM if smem and index == 0 else ANY if index in left else VMEM
            for index in range(len(operands))
        ],
        out_specs=[VMEM] * len(out),
        scratch_shapes=list(scratch),
        compiler_params=pltpu.CompilerParams(vmem_limit_bytes=24 * 2**20),
        cost_estimate=pl.CostEstimate(
            flops=4 * keys * query_rows * width,
            bytes_accessed=2 * (keys + query_rows) * width + 8 * query_rows * width,
            transcendentals=keys * query_rows,
        ),
    )(*operands)


def held(rows, width):
    return [
        jax.ShapeDtypeStruct((rows, 1), jnp.float32),
        jax.ShapeDtypeStruct((rows, 1), jnp.float32),
        jax.ShapeDtypeStruct((rows, width), jnp.float32),
    ]


def finish_kernel(
    score_scale, here_stat_ref, half_stat_ref, pair_ref,
    near_early_ref, near_late_ref, far_early_ref, far_late_ref, blended_ref, margin_ref,
):
    rows, early = blended_ref.shape[0], near_early_ref.shape[0]
    late = rows - early

    def merged(one, two):
        top = jnp.maximum(one[0], two[0])
        left = one[1] * jnp.exp2((one[0] - top) * (score_scale * LOG2_E))
        right = two[1] * jnp.exp2((two[0] - top) * (score_scale * LOG2_E))
        total = left + right
        return left / total, right / total, top * score_scale + jnp.log(total)

    near_tile, far_tile = near_late_ref[late:, :rows], far_late_ref[late:, :rows]
    near_share, far_share, own_log = merged(
        [of_threes(near_tile, index) for index in range(2)],
        [of_threes(far_tile, index) for index in range(2)],
    )
    there_log = merged(
        [here_stat_ref[index : index + 1, :] for index in range(2)],
        [half_stat_ref[index : index + 1, :] for index in range(2)],
    )[2]
    margin_ref[...] = pair_ref[...] - 0.5 * (own_log + there_log)
    near_share, far_share = near_share.T, far_share.T
    for here, count, near_ref, far_ref in (
        (slice(0, early), early, near_early_ref, far_early_ref),
        (slice(early, rows), late, near_late_ref, far_late_ref),
    ):
        blended_ref[here, :] = (
            near_ref[:count, :].astype(jnp.float32) * near_share[here, :]
            + far_ref[:count, :].astype(jnp.float32) * far_share[here, :]
        ).astype(jnp.bfloat16)


def after(value, *others):
    return lax.optimization_barrier((value, *others))[0]


def shards(embeddings, block_mask):
    own = embeddings[0]
    rows, width = own.shape
    early, late = parts_of(rows)
    score_scale = sharpness / math.sqrt(width)
    line = jax.ShapeDtypeStruct((1, rows), jnp.float32)

    near = moved(own, across_near)
    far = moved(own, across_far)
    own_sib = moved(own, sibling)
    first_1, second_1 = moved(own, onward), moved(own_sib, onward)
    first_2, second_2 = moved(first_1, onward), moved(second_1, onward)
    first_1_sib, second_1_sib = moved(after(first_1, near), sibling), moved(after(second_1, near), sibling)
    *state, queries = call(
        functools.partial(first_kernel, score_scale),
        held(2 * rows, width) + [jax.ShapeDtypeStruct((2 * rows, width), jnp.bfloat16)],
        [near, far, own, own_sib],
        scratch=[pltpu.VMEM(own.shape, own.dtype), pltpu.SemaphoreType.DMA(())],
        left=(2,),
    )
    first_2, state = lax.optimization_barrier((first_2, state))
    first_2_sib = moved(first_2, sibling)
    state = call(
        functools.partial(middle_kernel, score_scale, (1, 1, -1, -1)),
        held(2 * rows, width),
        [block_mask, queries, *state, first_1, second_1, first_1_sib, second_1_sib],
        smem=True,
    )
    second_2, state = lax.optimization_barrier((second_2, state))
    second_2_sib = moved(second_2, sibling)
    ring_2 = [first_2, first_2_sib, second_2, second_2_sib]
    early_state = call(
        functools.partial(middle_kernel, score_scale, (2, -2)),
        held(2 * early, width),
        [block_mask, queries, *state, *ring_2[:2]],
        keys=2 * rows, query_rows=2 * early, smem=True,
    )
    stats, sent = [], []
    for size, offsets, keys, source in (
        (early, (2, -2), ring_2[2:], early_state),
        (late, (2, -2, 2, -2), ring_2, state),
    ):
        near_part, far_part, *stats = call(
            functools.partial(last_kernel, score_scale, bool(sent), offsets),
            [jax.ShapeDtypeStruct((size + (16 if sent else 0), width), jnp.bfloat16)] * 2
            + [jax.ShapeDtypeStruct((2, rows if sent else size), jnp.float32)] * 2,
            [block_mask, queries, *source, *keys, *stats],
            scratch=[pltpu.VMEM(a.shape, a.dtype) for a in held(2 * rows, width)],
            keys=len(keys) * rows, query_rows=2 * size, smem=True,
        )
        sent.append((moved(near_part, across_near), moved(far_part, across_far)))
    near_stat, far_stat = stats
    pair_score = call(
        functools.partial(pair_kernel, score_scale), [line], [after(near, near_stat), own]
    )[0]
    blended, margin = call(
        functools.partial(finish_kernel, score_scale),
        [jax.ShapeDtypeStruct((rows, width), jnp.bfloat16), line],
        [
            near_stat,
            moved(far_stat, other_half),
            pair_score,
            sent[0][0], sent[1][0], sent[0][1], sent[1][1],
        ],
    )
    return (blended[None], margin)


def solution(mesh):
    placed = (P("dir", ("loop", "pb"), None), P())
    return jax.shard_map(
        shards,
        mesh=mesh,
        in_specs=placed,
        out_specs=(P("dir", ("loop", "pb"), None), P("dir", ("loop", "pb"))),
        check_vma=False,
    )
```

```python
import functools
import math

import jax
import jax.numpy as jnp
from jax import lax
from jax.experimental import pallas as pl
from jax.experimental.pallas import tpu as pltpu
from jax.sharding import PartitionSpec as P

sharpness = 3.0
AXES = ("dir", "loop", "pb")
LOG2_E = math.log2(math.e)
VMEM = pl.BlockSpec(memory_space=pltpu.VMEM)
SMEM = pl.BlockSpec(memory_space=pltpu.SMEM)
ANY = pl.BlockSpec(memory_space=pl.ANY)


def moved(value, route):
    sides, blocks, slabs = (lax.axis_size(axis) for axis in AXES)
    pairs = []
    for side in range(sides):
        for block in range(blocks):
            for slab in range(slabs):
                half, core = divmod(slab, 2)
                side_to, block_to, half_to, core_to = route(side, block, half, core)
                target = (side_to * blocks + block_to % blocks) * slabs + half_to * 2 + core_to
                pairs.append(((side * blocks + block) * slabs + slab, target))
    return lax.ppermute(value, AXES, pairs)


def across_near(side, block, half, core):
    return 1 - side, block, half, core


def across_far(side, block, half, core):
    return 1 - side, block, 1 - half, core


def other_half(side, block, half, core):
    return side, block, 1 - half, core


def sibling(side, block, half, core):
    return side, block, half, 1 - core


def onward(side, block, half, core):
    return side, block + (1 if core == 0 else -1), half, core


def key_bias(mask_ref, offsets, rows):
    side, block = lax.axis_index("dir"), lax.axis_index("loop")
    sign = jnp.where(lax.axis_index("pb") % 2 == 0, -1, 1)
    blocks = mask_ref.shape[0]
    column = lax.broadcasted_iota(jnp.int32, (1, rows * len(offsets)), 1)
    bias = jnp.zeros(column.shape, jnp.float32)
    for index, offset in enumerate(offsets):
        target = lax.rem(block + offset * sign + blocks, blocks)
        flag = jnp.where(side == 1, mask_ref[block, target], mask_ref[target, block])
        here = (column >= index * rows) & (column < (index + 1) * rows)
        bias = jnp.where(here & (flag <= 0), -jnp.inf, bias)
    return bias


def flash(query_ref, key_refs, score_scale, bias, state, out, begin, chunk, chunks):
    keys = jnp.concatenate([ref[...] for ref in key_refs], axis=0)
    heres = [pl.ds(begin + index * chunk, chunk) for index in range(chunks)]
    max_ref, total_ref, sum_ref = out

    def scored(here):
        scores = lax.dot_general(
            query_ref[here, :], keys, (((1,), (1,)), ((), ())), preferred_element_type=jnp.float32
        )
        return scores if bias is None else scores + bias

    ahead = scored(heres[0])
    for index, here in enumerate(heres):
        scores = ahead
        if index + 1 < chunks:
            ahead = scored(heres[index + 1])
        new_max = jnp.max(scores, axis=1, keepdims=True)
        if state:
            old_max = state[0][here, :]
            new_max = jnp.maximum(old_max, new_max)
        weights = jnp.exp2((scores - new_max) * (score_scale * LOG2_E))
        total = jnp.sum(weights, axis=1, keepdims=True)
        blended = jnp.dot(weights.astype(jnp.bfloat16), keys, preferred_element_type=jnp.float32)
        if state:
            correction = jnp.exp2((old_max - new_max) * (score_scale * LOG2_E))
            total += state[1][here, :] * correction
            blended += state[2][here, :] * correction
        max_ref[here, :] = new_max
        total_ref[here, :] = total
        sum_ref[here, :] = blended


def parts_of(rows):
    return rows - rows // 3, rows // 3


def first_kernel(
    score_scale, near_ref, far_ref, own_ref, sibling_ref,
    max_ref, total_ref, sum_ref, query_ref, held_ref, copy_sem,
):
    rows = own_ref.shape[0]
    early, late = parts_of(rows)
    copy = pltpu.make_async_copy(own_ref, held_ref, copy_sem)
    copy.start()
    query_ref[:early, :] = near_ref[:early, :]
    query_ref[early : 2 * early, :] = far_ref[:early, :]
    query_ref[2 * early : 2 * early + late, :] = near_ref[early:, :]
    query_ref[2 * early + late :, :] = far_ref[early:, :]
    copy.wait()
    flash(
        query_ref, (held_ref, sibling_ref), score_scale, None, None,
        (max_ref, total_ref, sum_ref), 0, rows, 2,
    )


def pair_kernel(score_scale, near_ref, own_ref, pair_ref):
    pair_ref[...] = (
        jnp.sum(
            near_ref[...].astype(jnp.float32) * own_ref[...].astype(jnp.float32),
            axis=1,
            keepdims=True,
        )
        * score_scale
    ).T


def middle_kernel(score_scale, offsets, mask_ref, query_ref, *refs):
    state, key_refs, out = refs[:3], refs[3:-3], refs[-3:]
    bias = key_bias(mask_ref, offsets, query_ref.shape[0] // 2)
    flash(query_ref, key_refs, score_scale, bias, state, out, 0, out[0].shape[0] // 2, 2)


def in_threes(lines):
    row = lax.broadcasted_iota(jnp.int32, (16, lines.shape[1]), 0)
    tile = jnp.zeros(row.shape, jnp.float32)
    for index in range(lines.shape[0]):
        line = lines[index : index + 1, :]
        high = line.astype(jnp.bfloat16).astype(jnp.float32)
        middle = (line - high).astype(jnp.bfloat16).astype(jnp.float32)
        for place, piece in enumerate((high, middle, line - high - middle)):
            tile = jnp.where(row == 3 * index + place, piece, tile)
    return tile.astype(jnp.bfloat16)


def of_threes(tile, index):
    high, middle, low = (
        tile[3 * index + place : 3 * index + place + 1, :].astype(jnp.float32)
        for place in range(3)
    )
    return low + middle + high


def last_kernel(score_scale, late, offsets, mask_ref, query_ref, *refs):
    count = len(offsets)
    state, key_refs, refs = refs[:3], refs[3 : 3 + count], list(refs[3 + count :])
    early_stats = [refs.pop(0), refs.pop(0)] if late else []
    near_ref, far_ref, near_stat_ref, far_stat_ref = refs[:4]
    out = refs[4:]
    rows = near_ref.shape[0] - (16 if late else 0)
    start = query_ref.shape[0] - 2 * rows if late else 0
    bias = key_bias(mask_ref, offsets, key_refs[0].shape[0])
    chunks = 1 if late else 2
    flash(query_ref, key_refs, score_scale, bias, state, out, start, 2 * rows // chunks, chunks)
    max_ref, total_ref, sum_ref = out
    for index, (part_ref, stat_ref) in enumerate(
        ((near_ref, near_stat_ref), (far_ref, far_stat_ref))
    ):
        these = pl.ds(start + index * rows, rows)
        total = total_ref[these, :]
        part_ref[:rows, :] = (sum_ref[these, :] / total).astype(jnp.bfloat16)
        early = early_stats[index].shape[1] if late else 0
        stat_ref[0:1, early:] = max_ref[these, :].T
        stat_ref[1:2, early:] = total.T
        if late:
            stat_ref[:, :early] = early_stats[index][...]
            part_ref[rows:, :] = jnp.zeros((16, part_ref.shape[1]), jnp.bfloat16)
            part_ref[rows:, : early + rows] = in_threes(stat_ref[...])


def call(kernel, out, operands, scratch=(), keys=0, query_rows=0, smem=False, left=()):
    width = max(operand.shape[1] for operand in operands)
    return pl.pallas_call(
        kernel,
        out_shape=out,
        in_specs=[
            SMEM if smem and index == 0 else ANY if index in left else VMEM
            for index in range(len(operands))
        ],
        out_specs=[VMEM] * len(out),
        scratch_shapes=list(scratch),
        compiler_params=pltpu.CompilerParams(vmem_limit_bytes=24 * 2**20),
        cost_estimate=pl.CostEstimate(
            flops=4 * keys * query_rows * width,
            bytes_accessed=2 * (keys + query_rows) * width + 8 * query_rows * width,
            transcendentals=keys * query_rows,
        ),
    )(*operands)


def held(rows, width):
    return [
        jax.ShapeDtypeStruct((rows, 1), jnp.float32),
        jax.ShapeDtypeStruct((rows, 1), jnp.float32),
        jax.ShapeDtypeStruct((rows, width), jnp.float32),
    ]


def finish_kernel(
    score_scale, here_stat_ref, half_stat_ref, pair_ref,
    near_early_ref, near_late_ref, far_early_ref, far_late_ref, blended_ref, margin_ref,
):
    rows, early = blended_ref.shape[0], near_early_ref.shape[0]
    late = rows - early

    def merged(one, two):
        top = jnp.maximum(one[0], two[0])
        left = one[1] * jnp.exp2((one[0] - top) * (score_scale * LOG2_E))
        right = two[1] * jnp.exp2((two[0] - top) * (score_scale * LOG2_E))
        total = left + right
        return left / total, right / total, top * score_scale + jnp.log(total)

    near_tile, far_tile = near_late_ref[late:, :rows], far_late_ref[late:, :rows]
    near_share, far_share, own_log = merged(
        [of_threes(near_tile, index) for index in range(2)],
        [of_threes(far_tile, index) for index in range(2)],
    )
    there_log = merged(
        [here_stat_ref[index : index + 1, :] for index in range(2)],
        [half_stat_ref[index : index + 1, :] for index in range(2)],
    )[2]
    margin_ref[...] = pair_ref[...] - 0.5 * (own_log + there_log)
    near_share, far_share = near_share.T, far_share.T
    for here, count, near_ref, far_ref in (
        (slice(0, early), early, near_early_ref, far_early_ref),
        (slice(early, rows), late, near_late_ref, far_late_ref),
    ):
        blended_ref[here, :] = (
            near_ref[:count, :].astype(jnp.float32) * near_share[here, :]
            + far_ref[:count, :].astype(jnp.float32) * far_share[here, :]
        ).astype(jnp.bfloat16)


def after(value, *others):
    return lax.optimization_barrier((value, *others))[0]


def shards(embeddings, block_mask):
    own = embeddings[0]
    rows, width = own.shape
    early, late = parts_of(rows)
    score_scale = sharpness / math.sqrt(width)
    line = jax.ShapeDtypeStruct((1, rows), jnp.float32)

    near = moved(own, across_near)
    far = moved(own, across_far)
    own_sib = moved(own, sibling)
    first_1, second_1 = moved(own, onward), moved(own_sib, onward)
    first_2, second_2 = moved(first_1, onward), moved(second_1, onward)
    first_1_sib, second_1_sib = moved(after(first_1, near), sibling), moved(after(second_1, near), sibling)
    *state, queries = call(
        functools.partial(first_kernel, score_scale),
        held(2 * rows, width) + [jax.ShapeDtypeStruct((2 * rows, width), jnp.bfloat16)],
        [near, far, own, own_sib],
        scratch=[pltpu.VMEM(own.shape, own.dtype), pltpu.SemaphoreType.DMA(())],
        left=(2,),
    )
    state = call(
        functools.partial(middle_kernel, score_scale, (1, 1, -1, -1)),
        held(2 * rows, width),
        [block_mask, queries, *state, first_1, second_1, first_1_sib, second_1_sib],
        smem=True,
    )
    first_2, second_2 = after(first_2, state[0]), after(second_2, state[0])
    first_2_sib = moved(first_2, sibling)
    second_2_sib = moved(second_2, sibling)
    ring_2 = [first_2, first_2_sib, second_2, second_2_sib]
    early_state = call(
        functools.partial(middle_kernel, score_scale, (2, -2)),
        held(2 * early, width),
        [block_mask, queries, *state, *ring_2[:2]],
        keys=2 * rows, query_rows=2 * early, smem=True,
    )
    stats, sent = [], []
    for size, offsets, keys, source in (
        (early, (2, -2), ring_2[2:], early_state),
        (late, (2, -2, 2, -2), ring_2, state),
    ):
        near_part, far_part, *stats = call(
            functools.partial(last_kernel, score_scale, bool(sent), offsets),
            [jax.ShapeDtypeStruct((size + (16 if sent else 0), width), jnp.bfloat16)] * 2
            + [jax.ShapeDtypeStruct((2, rows if sent else size), jnp.float32)] * 2,
            [block_mask, queries, *source, *keys, *stats],
            scratch=[pltpu.VMEM(a.shape, a.dtype) for a in held(2 * rows, width)],
            keys=len(keys) * rows, query_rows=2 * size, smem=True,
        )
        sent.append((moved(near_part, across_near), moved(far_part, across_far)))
    near_stat, far_stat = stats
    pair_score = call(
        functools.partial(pair_kernel, score_scale), [line], [after(near, near_stat), own]
    )[0]
    blended, margin = call(
        functools.partial(finish_kernel, score_scale),
        [jax.ShapeDtypeStruct((rows, width), jnp.bfloat16), line],
        [
            near_stat,
            moved(far_stat, other_half),
            pair_score,
            sent[0][0], sent[1][0], sent[0][1], sent[1][1],
        ],
    )
    return (blended[None], margin)


def solution(mesh):
    placed = (P("dir", ("loop", "pb"), None), P())
    return jax.shard_map(
        shards,
        mesh=mesh,
        in_specs=placed,
        out_specs=(P("dir", ("loop", "pb"), None), P("dir", ("loop", "pb"))),
        check_vma=False,
    )
```
